32 devices in a mesh: kv: 2 (over y), pb: 4 (over x, core), head: 4 (over z).
Axes of the slice: x: 2, y: 2, z: 4, core: 2. Of those that a mesh axis runs over, the one named last changes fastest.
Arguments:
- queries: bfloat16 [8192, 8192], P(('kv', 'pb', 'head')), may hold values from -20 to 20
- key_rows: bfloat16 [8192, 1024], P(('kv', 'pb', 'head')), may hold values from -5 to 5
- value_rows: bfloat16 [8192, 1024], P(('kv', 'pb', 'head')), may hold values from -6 to 6
- tile_lists: int32 [64, 8], P(('kv', 'pb')), may hold values from 0 to 63, as said below
Outputs:
- attended: bfloat16 [8192, 8192], P(('kv', 'pb', 'head'))
The draws below stay inside these ranges and needn't reach their ends.
Inputs may be any that keep to these rules, and one draw needn't show every extreme that they name: `tile_lists`: row i names min(i + 1, 8) distinct tiles in its first slots, all at most i, the first of them i itself; its other slots hold 0.
All inputs are finite; a program needn't handle non-finite values.
Results may differ from the reference program's by a relative error of at most 0.0042.
Values may be sent and summed in bfloat16 or wider, within the bound.
No kernel may reach another device: no remote copies, remote signals or barrier semaphores. Data moves between devices by JAX's collectives and lax.ppermute only.
A program may use at most 128 MiB of HBM per device.

```python
import jax
import jax.numpy as jnp
from jax import lax

HEADS = 64
KV_HEADS = 8
HEAD_DIM = 128
TILE = 128
SLOTS = 8
SEQ = 8192
QT = 64


def draw_queries(key, part):
    own_key = jax.random.fold_in(key, 11)
    base = jnp.clip(jax.random.normal(own_key, (SEQ, HEADS * HEAD_DIM), jnp.float32), -4.5, 4.5)
    return base.astype(jnp.bfloat16)


def draw_key_rows(key, part):
    own_key = jax.random.fold_in(key, 13)
    base = jnp.clip(jax.random.normal(own_key, (SEQ, KV_HEADS * HEAD_DIM), jnp.float32), -4.5, 4.5)
    return base.astype(jnp.bfloat16)


def draw_tile_lists(key, part):
    widest = max(QT, SLOTS)
    rows_index = jnp.arange(QT, dtype=jnp.int32)[:, None]
    column = jnp.arange(widest, dtype=jnp.int32)[None, :]
    ranks = jax.random.randint(jax.random.fold_in(key, 17), (QT, widest), 0, 1 << 20, dtype=jnp.int32)
    ranks = ranks * widest + column
    ranks = jnp.where(column == rows_index, jnp.int32(1 << 30), ranks)
    ranks = jnp.where(column > rows_index, -1 - column, ranks)
    picked = jax.lax.top_k(ranks, SLOTS)[1].astype(jnp.int32)
    active = jnp.minimum(rows_index + 1, SLOTS)
    slot_order = jnp.arange(SLOTS, dtype=jnp.int32)[None, :]
    return jnp.where(slot_order < active, picked, 0).astype(jnp.int32)


def shard_levels(key, dims, pieces, smallest, largest):
    def one(dim, blocks):
        heights = jax.random.uniform(jax.random.fold_in(jax.random.fold_in(key, 6), dim), (blocks,), jnp.float32, smallest / len(pieces), largest / len(pieces))
        return jnp.repeat(jnp.exp(heights), dims[dim] // blocks).reshape((-1,) + (1,) * (len(dims) - dim - 1))

    loudness = one(*pieces[0])
    for cut in pieces[1:]:
        loudness = loudness * one(*cut)
    return loudness


def noise(rng, shape, spread, most, shards=(), kind=jnp.bfloat16):
    entries = spread * jax.random.normal(rng, shape, jnp.float32)
    if shards:
        entries = entries * shard_levels(rng, shape, shards, -0.22, 0.18)
    return jnp.clip(entries, -most, most).astype(kind)


def setup_inputs(seed: int = 0) -> dict:
    seeds = jax.random.split(jax.random.key(seed), 5)
    queries = draw_queries(jax.random.fold_in(seeds[4], 71), 0)
    key_rows = draw_key_rows(jax.random.fold_in(seeds[4], 71), 0)
    value_rows = noise(seeds[2], (SEQ, KV_HEADS * HEAD_DIM), 1.0, 6.0, ((0, 32),))
    tile_lists = draw_tile_lists(jax.random.fold_in(seeds[4], 71), 0)
    return dict(queries=queries, key_rows=key_rows, value_rows=value_rows, tile_lists=tile_lists)


NEG = -1e30


def tile_partial(query_tile, key_tiles, value_tiles, allowed, scaling):
    scores = jnp.einsum("tkgd,jskd->tkgjs", query_tile.astype(jnp.float32), key_tiles.astype(jnp.float32)) * scaling
    scores = jnp.where(allowed[:, None, None, :, :], scores, NEG)
    tile_max = jnp.max(scores, axis=-1)
    weights = jnp.exp(scores - tile_max[..., None])
    tile_sum = jnp.sum(weights, axis=-1)
    rounded = lax.optimization_barrier(weights.astype(jnp.bfloat16))
    tile_out = jnp.einsum("tkgjs,jskd->tkgjd", rounded.astype(jnp.float32), value_tiles.astype(jnp.float32))
    return tile_max, tile_sum, tile_out


def combine_slots(tile_max, tile_sum, tile_out, usable):
    masked = jnp.where(usable, tile_max, NEG)
    overall = jnp.max(masked, axis=-1, keepdims=True)
    factor = jnp.exp(masked - overall)
    run_sum = jnp.sum(factor * tile_sum, axis=-1)
    run_out = jnp.sum(factor[..., None] * tile_out, axis=-2)
    return run_out / run_sum[..., None]


def reference(queries, key_rows, value_rows, tile_lists):
    groups = HEADS // KV_HEADS
    scaling = HEAD_DIM ** -0.5
    query_grid = queries.reshape(QT, TILE, KV_HEADS, groups, HEAD_DIM)
    key_grid = key_rows.reshape(QT, TILE, KV_HEADS, HEAD_DIM)
    value_grid = value_rows.reshape(QT, TILE, KV_HEADS, HEAD_DIM)
    within = jnp.arange(TILE, dtype=jnp.int32)
    slot_order = jnp.arange(SLOTS, dtype=jnp.int32)

    def one_tile(tile_index):
        listed = tile_lists[tile_index]
        key_tiles = jnp.take(key_grid, listed, axis=0)
        value_tiles = jnp.take(value_grid, listed, axis=0)
        query_position = tile_index * TILE + within
        key_position = listed[:, None] * TILE + within[None, :]
        allowed = key_position[None, :, :] <= query_position[:, None, None]
        usable = slot_order < jnp.minimum(tile_index + 1, SLOTS)
        tile_max, tile_sum, tile_out = tile_partial(query_grid[tile_index], key_tiles, value_tiles, allowed, scaling)
        return combine_slots(tile_max, tile_sum, tile_out, usable).astype(jnp.bfloat16)

    result = lax.map(one_tile, jnp.arange(QT, dtype=jnp.int32))
    return result.reshape(QT * TILE, HEADS * HEAD_DIM)
```

```python
import functools

import jax
import jax.numpy as jnp
from jax import lax
from jax.experimental import pallas as pl
from jax.experimental.pallas import tpu as pltpu
from jax.sharding import PartitionSpec as P

HEADS = 64
KV_HEADS = 8
HEAD_DIM = 128
TILE = 128
SLOTS = 8

NEG = -1e30
GROUPS = HEADS // KV_HEADS
WIDE = GROUPS * HEAD_DIM
AXES = ("kv", "pb", "head")
LOG2 = HEAD_DIM ** (-0.5) * 1.4426950408889634


def attend_tile(masked, live, tile, loc_ref, q_buf, kv_buf, out_buf):
    listed = [kv_buf[loc_ref[tile * SLOTS + j]] for j in range(SLOTS)]
    keys = jnp.concatenate([block[:, :HEAD_DIM] for block in listed], axis=0)
    values = jnp.concatenate([block[:, HEAD_DIM:] for block in listed], axis=0)
    values = jnp.concatenate([values, jnp.ones_like(values)], axis=1)
    row = lax.broadcasted_iota(jnp.int32, (TILE, TILE), 0)
    column = lax.broadcasted_iota(jnp.int32, (TILE, TILE), 1)
    diagonal = jnp.where(column <= row, 0.0, NEG)
    for g in range(GROUPS):
        columns = slice(g * HEAD_DIM, (g + 1) * HEAD_DIM)
        scores = lax.dot_general(
            q_buf[tile, :, columns], keys, (((1,), (1,)), ((), ())),
            preferred_element_type=jnp.float32,
        )
        parts = [scores[:, :TILE] + diagonal]
        if masked:
            for j in range(1, SLOTS):
                part = scores[:, j * TILE:(j + 1) * TILE]
                parts.append(part + jnp.where(j < live, 0.0, NEG))
        else:
            parts.append(scores[:, TILE:])
        scores = jnp.concatenate(parts, axis=1)
        top = jnp.max(scores, axis=1, keepdims=True)
        weights = jnp.exp2((scores - top) * LOG2).astype(jnp.bfloat16)
        total = jnp.dot(weights, values, preferred_element_type=jnp.float32)
        out_buf[tile, :, columns] = (total[:, :HEAD_DIM] / total[:, HEAD_DIM:]).astype(jnp.bfloat16)


def attend_kernel(blocks, tiles, sources, loc_ref, tid_ref, z_ref, *refs):
    q_refs, refs = refs[:blocks], refs[blocks:]
    kv_refs, refs = refs[:len(sources)], refs[len(sources):]
    out_refs, (q_buf, kv_buf, out_buf, q_sem, kv_sem, out_sem) = refs[:blocks], refs[blocks:]
    z = z_ref[0]

    def kv_copies(act):
        for i, (at, low, high) in enumerate(sources):
            rows = kv_refs[i].shape[0]
            start = at(z) * rows if at is not None else 0

            def one(i=i, start=start, rows=rows):
                copy = pltpu.make_async_copy(
                    kv_refs[i], kv_buf.at[pl.ds(start, rows)], kv_sem.at[i]
                )
                getattr(copy, act)()

            if low is None:
                one()
            else:
                pl.when(jnp.logical_and(z >= low, z <= high))(one)

    q_copies = [
        pltpu.make_async_copy(q_refs[i], q_buf.at[pl.ds(i * tiles, tiles)], q_sem.at[i])
        for i in range(blocks)
    ]
    for copy in q_copies:
        copy.start()
    kv_copies("start")
    for copy in q_copies:
        copy.wait()
    kv_copies("wait")

    def one_tile(tile, _):
        live = jnp.minimum(tid_ref[tile] + 1, SLOTS)

        @pl.when(live < SLOTS)
        def _():
            attend_tile(True, live, tile, loc_ref, q_buf, kv_buf, out_buf)

        @pl.when(live == SLOTS)
        def _():
            attend_tile(False, live, tile, loc_ref, q_buf, kv_buf, out_buf)

        return 0

    out_copies = [
        pltpu.make_async_copy(out_buf.at[pl.ds(i * tiles, tiles)], out_refs[i], out_sem.at[i])
        for i in range(blocks)
    ]
    for i in range(blocks):
        lax.fori_loop(i * tiles, (i + 1) * tiles, one_tile, 0)
        out_copies[i].start()
    for copy in out_copies:
        copy.wait()


def attend(q_blocks, kv_bufs, sources, kv_tiles, loc, tid, z):
    blocks = len(q_blocks)
    tiles = q_blocks[0].shape[0] // TILE
    q_blocks = [q.reshape(tiles, TILE, WIDE) for q in q_blocks]
    kv_bufs = [kv.reshape(-1, TILE, 2 * HEAD_DIM) for kv in kv_bufs]
    smem = pl.BlockSpec(memory_space=pltpu.SMEM)
    hbm = pl.BlockSpec(memory_space=pl.ANY)
    units = blocks * tiles
    out = pl.pallas_call(
        functools.partial(attend_kernel, blocks, tiles, sources),
        out_shape=[jax.ShapeDtypeStruct((tiles, TILE, WIDE), jnp.bfloat16)] * blocks,
        in_specs=[smem] * 3 + [hbm] * (blocks + len(kv_bufs)),
        out_specs=[hbm] * blocks,
        scratch_shapes=[
            pltpu.VMEM((units, TILE, WIDE), jnp.bfloat16),
            pltpu.VMEM((kv_tiles, TILE, 2 * HEAD_DIM), jnp.bfloat16),
            pltpu.VMEM((units, TILE, WIDE), jnp.bfloat16),
            pltpu.SemaphoreType.DMA((blocks,)),
            pltpu.SemaphoreType.DMA((len(kv_bufs),)),
            pltpu.SemaphoreType.DMA((blocks,)),
        ],
        compiler_params=pltpu.CompilerParams(vmem_limit_bytes=48 * 2**20),
        cost_estimate=pl.CostEstimate(
            flops=units * 4 * GROUPS * TILE * TILE * SLOTS * HEAD_DIM * 2,
            bytes_accessed=kv_tiles * TILE * 4 * HEAD_DIM + units * TILE * WIDE * 4,
            transcendentals=units * GROUPS * TILE * TILE * SLOTS,
        ),
    )(loc.reshape(-1), tid, z.reshape(1), *q_blocks, *kv_bufs)
    return [o.reshape(tiles * TILE, WIDE) for o in out]


def per_device(sizes, queries, key_rows, value_rows, tile_lists):
    kv_size, pb_size, z_size = sizes
    planes = kv_size * pb_size
    tokens = queries.shape[0]
    tiles = tokens // TILE
    z = lax.axis_index("head")
    pb = lax.axis_index("pb")
    kv = lax.axis_index("kv")
    b = kv * pb_size + pb

    def move(x, pairs):
        return lax.ppermute(x, AXES, pairs)

    def swap(x, offset, low=0, high=z_size - 1):
        return move(x, [
            (i * z_size + h, (i ^ offset) * z_size + h)
            for i in range(planes) for h in range(low, high + 1)
        ])

    lists = lax.all_gather(tile_lists, ("kv", "pb"), axis=0, tiled=True)

    relay = kv_size == 2 and pb_size == 4 and z_size <= 4
    sides = (2, 4) if relay else (2, 2)

    def head_of(half, offset):
        side = sides[half]
        mine = (b & 1) + 2 * ((b & side) // side)
        return 4 * half + (mine ^ ((offset & 1) + 2 * ((offset & side) // side)))

    def near(half):
        return (0, 1, sides[half], sides[half] + 1)

    kv_bufs, kv_sources = [], []
    for half in range(2):
        blocks = []
        for offset in near(half):
            at = head_of(half, offset) * HEAD_DIM
            piece = jnp.concatenate(
                [lax.dynamic_slice_in_dim(a, at, HEAD_DIM, axis=1) for a in (key_rows, value_rows)],
                axis=1,
            )
            blocks.append(swap(piece, offset) if offset else piece)
        own = jnp.concatenate(blocks, axis=0)
        if relay:
            across = 6 - sides[half]
            bufs, sources = [own, swap(own, across)], [(lambda z: z * 2, None, None), (lambda z: z * 2 + 1, None, None)]
            up = down = own
            for step in range(1, z_size):
                up = move(up, [
                    (i * z_size + h, i * z_size + h + 1)
                    for i in range(planes) for h in range(step - 1, z_size - 1)
                ])
                down = move(down, [
                    (i * z_size + h, i * z_size + h - 1)
                    for i in range(planes) for h in range(1, z_size - step + 1)
                ])
                for buf, shift, low, high in ((up, -step, step, z_size - 1), (down, step, 0, z_size - 1 - step)):
                    bufs += [buf, swap(buf, across, low, high)]
                    sources += [
                        (lambda z, shift=shift: (z + shift) * 2, low, high),
                        (lambda z, shift=shift: (z + shift) * 2 + 1, low, high),
                    ]
        else:
            bufs = [lax.all_gather(own, ("kv", "head"), axis=0, tiled=True)]
            sources = [(None, None, None)]
        kv_bufs.append(bufs)
        kv_sources.append(sources)

    def place(half, tile):
        device, within = tile // tiles, tile % tiles
        where, z_from = device // z_size, device % z_size
        differ = where ^ b
        side = sides[half]
        slot = (differ & 1) + 2 * ((differ & side) // side)
        if relay:
            across = 6 - side
            block = (z_from * 2 + (differ & across) // across) * 4 + slot
        else:
            block = ((where // pb_size) * z_size + z_from) * 4 + slot
        return block * tiles + within

    q_blocks = []
    for half in range(2):
        blocks = {}
        for offset in near(half):
            at = head_of(half, offset) * WIDE
            piece = lax.dynamic_slice_in_dim(queries, at, WIDE, axis=1)
            blocks[offset] = swap(piece, offset) if offset else piece
        q_blocks.append(blocks)

    result = jnp.zeros((tokens, HEADS * HEAD_DIM), jnp.bfloat16)
    for far in (True, False):
        for half in range(2):
            side = sides[half]
            offsets = (side + 1, side) if far else (1, 0)
            tid = jnp.concatenate([
                ((b ^ offset) * z_size + z) * tiles + jnp.arange(tiles, dtype=jnp.int32)
                for offset in offsets
            ])
            loc = place(half, jnp.take(lists, tid, axis=0))
            outs = attend(
                [q_blocks[half][offset] for offset in offsets],
                kv_bufs[half], kv_sources[half], planes * z_size * tiles, loc, tid, z,
            )
            for offset, out in zip(offsets, outs):
                back = swap(out, offset) if offset else out
                result = lax.dynamic_update_slice_in_dim(result, back, head_of(half, offset) * WIDE, axis=1)
    return result


def solution(mesh):
    in_specs = (P(AXES, None), P(AXES, None), P(AXES, None), P(("kv", "pb"), None))
    sizes = tuple(mesh.shape[axis] for axis in AXES)
    return jax.shard_map(
        functools.partial(per_device, sizes),
        mesh=mesh, in_specs=in_specs, out_specs=P(AXES, None), check_vma=False,
    )
```

```python
import functools

import jax
import jax.numpy as jnp
from jax import lax
from jax.experimental import pallas as pl
from jax.experimental.pallas import tpu as pltpu
from jax.sharding import PartitionSpec as P

HEADS = 64
KV_HEADS = 8
HEAD_DIM = 128
TILE = 128
SLOTS = 8

NEG = -1e30
GROUPS = HEADS // KV_HEADS
WIDE = GROUPS * HEAD_DIM
AXES = ("kv", "pb", "head")
LOG2 = HEAD_DIM ** (-0.5) * 1.4426950408889634


def attend_tile(masked, live, tile, loc_ref, q_buf, kv_buf, out_buf):
    listed = [kv_buf[loc_ref[tile * SLOTS + j]] for j in range(SLOTS)]
    keys = jnp.concatenate([block[:, :HEAD_DIM] for block in listed], axis=0)
    values = jnp.concatenate([block[:, HEAD_DIM:] for block in listed], axis=0)
    values = jnp.concatenate([values, jnp.ones_like(values)], axis=1)
    row = lax.broadcasted_iota(jnp.int32, (TILE, TILE), 0)
    column = lax.broadcasted_iota(jnp.int32, (TILE, TILE), 1)
    diagonal = jnp.where(column <= row, 0.0, NEG)
    for g in range(GROUPS):
        columns = slice(g * HEAD_DIM, (g + 1) * HEAD_DIM)
        scores = lax.dot_general(
            q_buf[tile, :, columns], keys, (((1,), (1,)), ((), ())),
            preferred_element_type=jnp.float32,
        )
        parts = [scores[:, :TILE] + diagonal]
        if masked:
            for j in range(1, SLOTS):
                part = scores[:, j * TILE:(j + 1) * TILE]
                parts.append(part + jnp.where(j < live, 0.0, NEG))
        else:
            parts.append(scores[:, TILE:])
        scores = jnp.concatenate(parts, axis=1)
        top = jnp.max(scores, axis=1, keepdims=True)
        weights = jnp.exp2((scores - top) * LOG2).astype(jnp.bfloat16)
        total = jnp.dot(weights, values, preferred_element_type=jnp.float32)
        out_buf[tile, :, columns] = (total[:, :HEAD_DIM] / total[:, HEAD_DIM:]).astype(jnp.bfloat16)


def attend_kernel(blocks, tiles, sources, loc_ref, tid_ref, z_ref, *refs):
    q_refs, refs = refs[:blocks], refs[blocks:]
    kv_refs, refs = refs[:len(sources)], refs[len(sources):]
    out_refs, (q_buf, kv_buf, out_buf, q_sem, kv_sem, out_sem) = refs[:blocks], refs[blocks:]
    z = z_ref[0]

    def kv_copies(act):
        for i, (at, places) in enumerate(sources):
            rows = kv_refs[i].shape[0]

            def one(i=i, at=at, rows=rows):
                copy = pltpu.make_async_copy(
                    kv_refs[i], kv_buf.at[pl.ds(at * rows, rows)], kv_sem.at[i]
                )
                getattr(copy, act)()

            if places is None:
                one()
            else:
                here = z == places[0]
                for place in places[1:]:
                    here = jnp.logical_or(here, z == place)
                pl.when(here)(one)

    q_copies = [
        pltpu.make_async_copy(q_refs[i], q_buf.at[pl.ds(i * tiles, tiles)], q_sem.at[i])
        for i in range(blocks)
    ]
    for copy in q_copies:
        copy.start()
    kv_copies("start")
    for copy in q_copies:
        copy.wait()
    kv_copies("wait")

    def one_tile(tile, _):
        live = jnp.minimum(tid_ref[tile] + 1, SLOTS)

        @pl.when(live < SLOTS)
        def _():
            attend_tile(True, live, tile, loc_ref, q_buf, kv_buf, out_buf)

        @pl.when(live == SLOTS)
        def _():
            attend_tile(False, live, tile, loc_ref, q_buf, kv_buf, out_buf)

        return 0

    out_copies = [
        pltpu.make_async_copy(out_buf.at[pl.ds(i * tiles, tiles)], out_refs[i], out_sem.at[i])
        for i in range(blocks)
    ]
    for i in range(blocks):
        lax.fori_loop(i * tiles, (i + 1) * tiles, one_tile, 0)
        out_copies[i].start()
    for copy in out_copies:
        copy.wait()


def attend(q_blocks, kv_bufs, sources, kv_tiles, loc, tid, z):
    blocks = len(q_blocks)
    tiles = q_blocks[0].shape[0] // TILE
    q_blocks = [q.reshape(tiles, TILE, WIDE) for q in q_blocks]
    kv_bufs = [kv.reshape(-1, TILE, 2 * HEAD_DIM) for kv in kv_bufs]
    smem = pl.BlockSpec(memory_space=pltpu.SMEM)
    hbm = pl.BlockSpec(memory_space=pl.ANY)
    units = blocks * tiles
    out = pl.pallas_call(
        functools.partial(attend_kernel, blocks, tiles, sources),
        out_shape=[jax.ShapeDtypeStruct((tiles, TILE, WIDE), jnp.bfloat16)] * blocks,
        in_specs=[smem] * 3 + [hbm] * (blocks + len(kv_bufs)),
        out_specs=[hbm] * blocks,
        scratch_shapes=[
            pltpu.VMEM((units, TILE, WIDE), jnp.bfloat16),
            pltpu.VMEM((kv_tiles, TILE, 2 * HEAD_DIM), jnp.bfloat16),
            pltpu.VMEM((units, TILE, WIDE), jnp.bfloat16),
            pltpu.SemaphoreType.DMA((blocks,)),
            pltpu.SemaphoreType.DMA((len(kv_bufs),)),
            pltpu.SemaphoreType.DMA((blocks,)),
        ],
        compiler_params=pltpu.CompilerParams(vmem_limit_bytes=48 * 2**20),
        cost_estimate=pl.CostEstimate(
            flops=units * 4 * GROUPS * TILE * TILE * SLOTS * HEAD_DIM * 2,
            bytes_accessed=kv_tiles * TILE * 4 * HEAD_DIM + units * TILE * WIDE * 4,
            transcendentals=units * GROUPS * TILE * TILE * SLOTS,
        ),
    )(loc.reshape(-1), tid, z.reshape(1), *q_blocks, *kv_bufs)
    return [o.reshape(tiles * TILE, WIDE) for o in out]


def per_device(sizes, queries, key_rows, value_rows, tile_lists):
    kv_size, pb_size, z_size = sizes
    planes = kv_size * pb_size
    tokens = queries.shape[0]
    tiles = tokens // TILE
    z = lax.axis_index("head")
    pb = lax.axis_index("pb")
    kv = lax.axis_index("kv")
    b = kv * pb_size + pb

    def swap(x, offset, places=tuple(range(z_size))):
        return lax.ppermute(x, AXES, [
            (i * z_size + h, (i ^ offset) * z_size + h) for i in range(planes) for h in places
        ])

    def along(x, pairs):
        return lax.ppermute(x, AXES, [
            (i * z_size + h, i * z_size + k) for i in range(planes) for h, k in pairs
        ])

    relay = kv_size == 2 and pb_size == 4 and z_size == 4
    sides = (2, 4) if relay else (2, 2)

    def head_of(half, offset):
        side = sides[half]
        mine = (b & 1) + 2 * ((b & side) // side)
        return 4 * half + (mine ^ ((offset & 1) + 2 * ((offset & side) // side)))

    def near(half):
        return (0, 1, sides[half], sides[half] + 1)

    own_lists = lax.dynamic_slice_in_dim(tile_lists, z * tiles, tiles, axis=0)
    rider = jnp.concatenate([own_lists % 128, own_lists // 128], axis=0).astype(jnp.bfloat16)
    rider = jnp.pad(rider, ((0, -(2 * tiles) % 16), (0, 2 * HEAD_DIM - SLOTS)))
    own, lists = [], []
    for half in range(2):
        blocks, riders = [], []
        for offset in near(half):
            at = head_of(half, offset) * HEAD_DIM
            piece = jnp.concatenate(
                [lax.dynamic_slice_in_dim(a, at, HEAD_DIM, axis=1) for a in (key_rows, value_rows)],
                axis=1,
            )
            piece = jnp.concatenate([piece, rider], axis=0)
            if offset:
                piece = swap(piece, offset)
            blocks.append(piece[:tokens])
            parts = piece[tokens:tokens + 2 * tiles, :SLOTS].astype(jnp.int32)
            riders.append(parts[:tiles] + 128 * parts[tiles:])
        own.append(jnp.concatenate(blocks, axis=0))
        lists.append(dict(zip(near(half), riders)))
    *own, queries = lax.optimization_barrier((*own, queries))

    kv_bufs, kv_sources = [[], []], [[], []]
    if relay:
        across = [6 - side for side in sides]

        def add(half, buf, distance, places=None):
            take = tuple(range(z_size)) if places is None else places
            kv_bufs[half] += [buf, swap(buf, across[half], take)]
            kv_sources[half] += [(distance * 2, places), (distance * 2 + 1, places)]

        two = [along(x, ((0, 2), (1, 3), (2, 0), (3, 1))) for x in own]
        one = [along(x, ((0, 1), (1, 0), (2, 3), (3, 2))) for x in own]
        for half in range(2):
            add(half, own[half], 0)
            add(half, one[half], 1)
            add(half, two[half], 2)
            outer = along(two[half], ((1, 0), (2, 3)))
            inner = along(own[half], ((1, 2), (2, 1)))
            add(half, outer, 3, (0, 3))
            add(half, inner, 3, (1, 2))
    else:
        for half in range(2):
            kv_bufs[half].append(lax.all_gather(own[half], ("kv", "head"), axis=0, tiled=True))
            kv_sources[half].append((0, None))

    def place(half, tile):
        device, within = tile // tiles, tile % tiles
        where, z_from = device // z_size, device % z_size
        differ = where ^ b
        side = sides[half]
        slot = (differ & 1) + 2 * ((differ & side) // side)
        if relay:
            block = ((z_from ^ z) * 2 + (differ & across[half]) // across[half]) * 4 + slot
        else:
            block = ((where // pb_size) * z_size + z_from) * 4 + slot
        return block * tiles + within

    q_blocks = []
    for half in range(2):
        blocks = {}
        for offset in near(half):
            at = head_of(half, offset) * WIDE
            piece = lax.dynamic_slice_in_dim(queries, at, WIDE, axis=1)
            blocks[offset] = swap(piece, offset) if offset else piece
        q_blocks.append(blocks)

    result = jnp.zeros((tokens, HEADS * HEAD_DIM), jnp.bfloat16)
    for far in (True, False):
        for half in range(2):
            side = sides[half]
            offsets = (side + 1, side) if far else (1, 0)
            tid = jnp.concatenate([
                ((b ^ offset) * z_size + z) * tiles + jnp.arange(tiles, dtype=jnp.int32)
                for offset in offsets
            ])
            loc = place(half, jnp.concatenate([lists[half][offset] for offset in offsets], axis=0))
            outs = attend(
                [q_blocks[half][offset] for offset in offsets],
                kv_bufs[half], kv_sources[half], planes * z_size * tiles, loc, tid, z,
            )
            for offset, out in zip(offsets, outs):
                back = swap(out, offset) if offset else out
                result = lax.dynamic_update_slice_in_dim(result, back, head_of(half, offset) * WIDE, axis=1)
    return result


def solution(mesh):
    in_specs = (P(AXES, None), P(AXES, None), P(AXES, None), P(("kv", "pb"), None))
    sizes = tuple(mesh.shape[axis] for axis in AXES)
    return jax.shard_map(
        functools.partial(per_device, sizes),
        mesh=mesh, in_specs=in_specs, out_specs=P(AXES, None), check_vma=False,
    )
```

```python
import functools

import jax
import jax.numpy as jnp
from jax import lax
from jax.experimental import pallas as pl
from jax.experimental.pallas import tpu as pltpu
from jax.sharding import PartitionSpec as P

HEADS = 64
KV_HEADS = 8
HEAD_DIM = 128
TILE = 128
SLOTS = 8

NEG = -1e30
GROUPS = HEADS // KV_HEADS
WIDE = GROUPS * HEAD_DIM
AXES = ("kv", "pb", "head")
LOG2 = HEAD_DIM ** (-0.5) * 1.4426950408889634


def attend_tile(masked, live, tile, loc_ref, q_buf, kv_buf, out_buf):
    listed = [kv_buf[loc_ref[tile * SLOTS + j]] for j in range(SLOTS)]
    keys = jnp.concatenate([block[:, :HEAD_DIM] for block in listed], axis=0)
    values = jnp.concatenate([block[:, HEAD_DIM:] for block in listed], axis=0)
    values = jnp.concatenate([values, jnp.ones_like(values)], axis=1)
    row = lax.broadcasted_iota(jnp.int32, (TILE, TILE), 0)
    column = lax.broadcasted_iota(jnp.int32, (TILE, TILE), 1)
    diagonal = jnp.where(column <= row, 0.0, NEG)
    for g in range(GROUPS):
        columns = slice(g * HEAD_DIM, (g + 1) * HEAD_DIM)
        scores = lax.dot_general(
            q_buf[tile, :, columns], keys, (((1,), (1,)), ((), ())),
            preferred_element_type=jnp.float32,
        )
        parts = [scores[:, :TILE] + diagonal]
        if masked:
            for j in range(1, SLOTS):
                part = scores[:, j * TILE:(j + 1) * TILE]
                parts.append(part + jnp.where(j < live, 0.0, NEG))
        else:
            parts.append(scores[:, TILE:])
        scores = jnp.concatenate(parts, axis=1)
        top = jnp.max(scores, axis=1, keepdims=True)
        weights = jnp.exp2((scores - top) * LOG2).astype(jnp.bfloat16)
        total = jnp.dot(weights, values, preferred_element_type=jnp.float32)
        out_buf[tile, :, columns] = (total[:, :HEAD_DIM] / total[:, HEAD_DIM:]).astype(jnp.bfloat16)


def attend_kernel(blocks, tiles, starts, loc_ref, tid_ref, col_ref, *refs):
    q_refs, refs = refs[:blocks], refs[blocks:]
    kv_refs, refs = refs[:len(starts)], refs[len(starts):]
    out_refs, (q_buf, kv_buf, out_buf, q_sem, kv_sem, out_sem) = refs[:blocks], refs[blocks:]
    copies = [
        pltpu.make_async_copy(
            q_refs[i].at[:, :, pl.ds(pl.multiple_of(col_ref[i], WIDE), WIDE)],
            q_buf.at[pl.ds(i * tiles, tiles)], q_sem.at[i],
        )
        for i in range(blocks)
    ] + [
        pltpu.make_async_copy(
            kv_refs[i], kv_buf.at[pl.ds(start, kv_refs[i].shape[0])], kv_sem.at[i]
        )
        for i, start in enumerate(starts)
    ]
    for copy in copies:
        copy.start()
    for copy in copies:
        copy.wait()

    def one_tile(tile, _):
        live = jnp.minimum(tid_ref[tile] + 1, SLOTS)

        @pl.when(live < SLOTS)
        def _():
            attend_tile(True, live, tile, loc_ref, q_buf, kv_buf, out_buf)

        @pl.when(live == SLOTS)
        def _():
            attend_tile(False, live, tile, loc_ref, q_buf, kv_buf, out_buf)

        return 0

    out_copies = [
        pltpu.make_async_copy(out_buf.at[pl.ds(i * tiles, tiles)], out_refs[i], out_sem.at[i])
        for i in range(blocks)
    ]
    for i in range(blocks):
        lax.fori_loop(i * tiles, (i + 1) * tiles, one_tile, 0)
        out_copies[i].start()
    for copy in out_copies:
        copy.wait()


def attend(tiles, q_blocks, kv_bufs, loc, tid):
    blocks = len(q_blocks)
    queries = [q.reshape(tiles, TILE, -1) for q, _ in q_blocks]
    columns = jnp.stack([jnp.asarray(at, jnp.int32) for _, at in q_blocks])
    kv_bufs = [kv.reshape(-1, TILE, 2 * HEAD_DIM) for kv in kv_bufs]
    starts, kv_tiles = [], 0
    for kv in kv_bufs:
        starts.append(kv_tiles)
        kv_tiles += kv.shape[0]
    smem = pl.BlockSpec(memory_space=pltpu.SMEM)
    hbm = pl.BlockSpec(memory_space=pl.ANY)
    units = blocks * tiles
    out = pl.pallas_call(
        functools.partial(attend_kernel, blocks, tiles, starts),
        out_shape=[jax.ShapeDtypeStruct((tiles, TILE, WIDE), jnp.bfloat16)] * blocks,
        in_specs=[smem] * 3 + [hbm] * (blocks + len(kv_bufs)),
        out_specs=[hbm] * blocks,
        scratch_shapes=[
            pltpu.VMEM((units, TILE, WIDE), jnp.bfloat16),
            pltpu.VMEM((kv_tiles, TILE, 2 * HEAD_DIM), jnp.bfloat16),
            pltpu.VMEM((units, TILE, WIDE), jnp.bfloat16),
            pltpu.SemaphoreType.DMA((blocks,)),
            pltpu.SemaphoreType.DMA((len(kv_bufs),)),
            pltpu.SemaphoreType.DMA((blocks,)),
        ],
        compiler_params=pltpu.CompilerParams(vmem_limit_bytes=32 * 2**20),
        cost_estimate=pl.CostEstimate(
            flops=units * 4 * GROUPS * TILE * TILE * SLOTS * HEAD_DIM * 2,
            bytes_accessed=kv_tiles * TILE * 4 * HEAD_DIM + units * TILE * WIDE * 4,
            transcendentals=units * GROUPS * TILE * TILE * SLOTS,
        ),
    )(loc.reshape(-1), tid, columns, *queries, *kv_bufs)
    return [o.reshape(tiles * TILE, WIDE) for o in out]


def per_device(sizes, queries, key_rows, value_rows, tile_lists):
    kv_size, pb_size, z_size = sizes
    planes = kv_size * pb_size
    tokens = queries.shape[0]
    tiles = tokens // TILE
    z = lax.axis_index("head")
    b = lax.axis_index("kv") * pb_size + lax.axis_index("pb")
    core = b & 1

    def swap(x, offset):
        return lax.ppermute(x, AXES, [
            (i * z_size + h, (i ^ offset) * z_size + h) for i in range(planes) for h in range(z_size)
        ])

    def along(x, pairs):
        return lax.ppermute(x, AXES, [
            (i * z_size + h, i * z_size + k) for i in range(planes) for h, k in pairs
        ])

    relay = kv_size == 2 and pb_size == 4 and z_size == 4
    sides = (2, 4) if relay else (2, 2)
    halves = range(2)

    def head_of(half, offset):
        side = sides[half]
        mine = core + 2 * ((b & side) // side)
        return 4 * half + (mine ^ ((offset & 1) + 2 * ((offset & side) // side)))

    def near(half):
        return (0, 1, sides[half], sides[half] + 1)

    own_lists = lax.dynamic_slice_in_dim(tile_lists, z * tiles, tiles, axis=0)
    rider = jnp.concatenate([own_lists % 128, own_lists // 128], axis=0).astype(jnp.bfloat16)
    rider = jnp.pad(rider, ((0, -(2 * tiles) % 16), (0, 2 * HEAD_DIM - SLOTS)))
    own, lists = [], []
    for half in halves:
        blocks, riders = [], []
        for offset in near(half):
            at = head_of(half, offset) * HEAD_DIM
            piece = jnp.concatenate(
                [lax.dynamic_slice_in_dim(a, at, HEAD_DIM, axis=1) for a in (key_rows, value_rows)],
                axis=1,
            )
            piece = jnp.concatenate([piece, rider], axis=0)
            if offset:
                piece = swap(piece, offset)
            blocks.append(piece[:tokens])
            parts = piece[tokens:tokens + 2 * tiles, :SLOTS].astype(jnp.int32)
            riders.append(parts[:tiles] + 128 * parts[tiles:])
        own.append(jnp.concatenate(blocks, axis=0))
        lists.append(dict(zip(near(half), riders)))
    *own, queries = lax.optimization_barrier((*own, queries))

    def columns(array, at, count=1):
        return lax.dynamic_slice_in_dim(array, at, count * WIDE, axis=1)

    def query_pair(half):
        return columns(queries, (head_of(half, sides[half]) - core) * WIDE, 2)

    def tie(*arrays):
        return lax.optimization_barrier(arrays)

    if relay:
        across = [6 - side for side in sides]
        middle = jnp.logical_or(z == 1, z == 2)
        by_two, by_one = ((0, 2), (1, 3), (2, 0), (3, 1)), ((0, 1), (1, 0), (2, 3), (3, 2))
        outward, inward = ((1, 0), (2, 3)), ((1, 2), (2, 1))
        own_a, own_b = own
        rows = own_a.shape[0]
        both = jnp.concatenate(own, axis=0)
        two, one = along(both, by_two), along(both, by_one)
        own_a_far, own_b_far = swap(own_a, across[0]), swap(own_b, across[1])
        crossed_a = swap(query_pair(0), sides[0])
        turned_b, own_a_far = tie(query_pair(1), own_a_far)
        crossed_b = swap(turned_b, sides[1])
        both, one, two, own_a, own_b, own_a_far, own_b_far, crossed_a, crossed_b = tie(
            both, one, two, own_a, own_b, own_a_far, own_b_far, crossed_a, crossed_b
        )
        crossed = [crossed_a, crossed_b]
        outer, inner = along(two, outward), along(both, inward)
        pair_a = jnp.concatenate([one[:rows], two[:rows]], axis=0)
        pair_b = jnp.concatenate([one[rows:], two[rows:]], axis=0)
        pair_a_far, pair_b_far = swap(pair_a, across[0]), swap(pair_b, across[1])
        outer, inner, pair_a, pair_b, pair_a_far, pair_b_far = tie(
            outer, inner, pair_a, pair_b, pair_a_far, pair_b_far
        )
        three = jnp.where(middle, inner, outer)
        three_a, three_b = three[:rows], three[rows:]
        kv_bufs = [
            [own_a, own_a_far, pair_a, pair_a_far, three_a, swap(three_a, across[0])],
            [own_b, own_b_far, pair_b, pair_b_far, three_b, swap(three_b, across[1])],
        ]
    else:
        kv_bufs = [[lax.all_gather(x, ("kv", "head"), axis=0, tiled=True)] for x in own]
        crossed = [swap(query_pair(half), sides[half]) for half in halves]

    def place(half, tile):
        device, within = tile // tiles, tile % tiles
        where, z_from = device // z_size, device % z_size
        differ = where ^ b
        side = sides[half]
        slot = (differ & 1) + 2 * ((differ & side) // side)
        if relay:
            distance, far = z_from ^ z, (differ & across[half]) // across[half]
            block = jnp.where(
                distance == 0, far, jnp.where(distance == 3, 6 + far, 1 + distance + 2 * far)
            )
        else:
            block = (where // pb_size) * z_size + z_from
        return (block * 4 + slot) * tiles + within

    other = 1 - core
    by_core = swap(jnp.concatenate([
        part for half in halves
        for part in (columns(queries, head_of(half, 1) * WIDE), columns(crossed[half], other * WIDE))
    ], axis=1), 1)

    result = jnp.zeros((tokens, HEADS * HEAD_DIM), jnp.bfloat16)
    for far in (True, False):
        for half in halves:
            side = sides[half]
            if far:
                offsets = (side + 1, side)
                q_blocks = [(by_core, (2 * half + 1) * WIDE), (crossed[half], core * WIDE)]
            else:
                offsets = (1, 0)
                q_blocks = [(by_core, 2 * half * WIDE), (queries, head_of(half, 0) * WIDE)]
            tid = jnp.concatenate([
                ((b ^ offset) * z_size + z) * tiles + jnp.arange(tiles, dtype=jnp.int32)
                for offset in offsets
            ])
            loc = place(half, jnp.concatenate([lists[half][offset] for offset in offsets], axis=0))
            outs = attend(tiles, q_blocks, kv_bufs[half], loc, tid)
            for offset, out in zip(offsets, outs):
                back = swap(out, offset) if offset else out
                result = lax.dynamic_update_slice_in_dim(result, back, head_of(half, offset) * WIDE, axis=1)
    return result


def solution(mesh):
    in_specs = (P(AXES, None), P(AXES, None), P(AXES, None), P(("kv", "pb"), None))
    sizes = tuple(mesh.shape[axis] for axis in AXES)
    return jax.shard_map(
        functools.partial(per_device, sizes),
        mesh=mesh, in_specs=in_specs, out_specs=P(AXES, None), check_vma=False,
    )
```

```python
import functools

import jax
import jax.numpy as jnp
from jax import lax
from jax.experimental import pallas as pl
from jax.experimental.pallas import tpu as pltpu
from jax.sharding import PartitionSpec as P

HEADS = 64
KV_HEADS = 8
HEAD_DIM = 128
TILE = 128
SLOTS = 8

NEG = -1e30
GROUPS = HEADS // KV_HEADS
WIDE = GROUPS * HEAD_DIM
VMEM_LIMIT = 60 * 2**20
AXES = ("kv", "pb", "head")
LOG2 = HEAD_DIM ** (-0.5) * 1.4426950408889634


def rows_of(tile, count=1):
    return pl.ds(pl.multiple_of(tile * TILE, TILE), count * TILE)


def attend_tiles(count, masked, first, tid_ref, q_buf, kv_buf, out_buf):
    keys, values = [], []
    for t in range(count):
        listed = rows_of((first + t) * SLOTS, SLOTS)
        keys.append(kv_buf[listed, :HEAD_DIM])
        value = kv_buf[listed, HEAD_DIM:]
        values.append(jnp.concatenate([value, jnp.ones_like(value)], axis=1))
    row = lax.broadcasted_iota(jnp.int32, (TILE, TILE), 0)
    column = lax.broadcasted_iota(jnp.int32, (TILE, TILE), 1)
    diagonal = jnp.where(column <= row, 0.0, NEG)

    def score(t, g):
        scores = lax.dot_general(
            q_buf[rows_of(first + t), g * HEAD_DIM:(g + 1) * HEAD_DIM], keys[t], (((1,), (1,)), ((), ())),
            preferred_element_type=jnp.float32,
        )
        parts = [scores[:, :TILE] + diagonal]
        if masked:
            live = tid_ref[first + t] + 1
            for j in range(1, SLOTS):
                part = scores[:, j * TILE:(j + 1) * TILE]
                parts.append(part + jnp.where(j < live, 0.0, NEG))
        else:
            parts.append(scores[:, TILE:])
        return jnp.concatenate(parts, axis=1)

    def weigh(scores):
        top = jnp.max(scores, axis=1, keepdims=True)
        return jnp.exp2((scores - top) * LOG2).astype(jnp.bfloat16)

    def finish(weights, t, g):
        total = jnp.dot(weights, values[t], preferred_element_type=jnp.float32)
        out = total[:, :HEAD_DIM] / total[:, HEAD_DIM:]
        out_buf[rows_of(first + t), g * HEAD_DIM:(g + 1) * HEAD_DIM] = out.astype(jnp.bfloat16)

    units = [(t, g) for t in range(count) for g in range(GROUPS)]
    ahead = 0 if masked else 3
    scores, weights = {}, {}
    for step in range(len(units) + ahead + 1):
        if step < len(units):
            scores[step] = score(*units[step])
        if 0 <= step - ahead < len(units):
            weights[step - ahead] = weigh(scores.pop(step - ahead))
        if step - ahead >= 1:
            finish(weights.pop(step - ahead - 1), *units[step - ahead - 1])


def attend_kernel(blocks, tiles, starts, direct, shared, pieces, turn_ref, loc_ref, tid_ref, col_ref, *refs):
    q_refs, refs = refs[:blocks], refs[blocks:]
    kv_refs, refs = refs[:len(starts)], refs[len(starts):]
    piece_refs, refs = refs[:pieces], refs[pieces:]
    out_refs, (next_ref, q_buf, kv_buf, out_buf, piece_buf, *sems) = refs[:-9], refs[-9:]
    q_sem, kv_sem, out_sem, piece_sem = sems
    next_ref[0] = turn_ref[0] + 1

    def wide(i):
        return pl.ds(pl.multiple_of(col_ref[i], WIDE), WIDE)

    q_copies = [
        pltpu.make_async_copy(
            q_refs[i].at[:, wide(i)], q_buf.at[rows_of(i * tiles, tiles)], q_sem.at[i]
        )
        for i in range(blocks)
    ]

    def fetch(slot, sem):
        at = loc_ref[slot]
        for ref, start in zip(kv_refs, starts):
            here = at - start

            @pl.when(jnp.logical_and(here >= 0, here < ref.shape[0] // TILE))
            def _(ref=ref, here=here):
                pltpu.make_async_copy(ref.at[rows_of(here)], kv_buf.at[rows_of(slot)], sem).start()

    def fetch_block(i):
        slots = tiles * SLOTS
        for k, copy in enumerate(q_copies):
            pl.when(i == k)(copy.start)

        def one_slot(slot, _):
            fetch(slot, kv_sem.at[i])
            return 0

        lax.fori_loop(i * slots, (i + 1) * slots, one_slot, 0)

    fetch_block(0)
    piece_ins, piece_outs = [], []
    for i in range(pieces):
        buf = piece_buf.at[rows_of(i * tiles, tiles)]
        piece_ins.append(pltpu.make_async_copy(piece_refs[i], buf, piece_sem.at[i]))
        piece_outs.append(
            pltpu.make_async_copy(buf, out_refs[0].at[:, wide(2 * blocks + i)], out_sem.at[blocks + i])
        )
        piece_ins[-1].start()

    out_copies = []
    for i in range(blocks):
        alone = blocks - shared
        if direct:
            target = out_refs[0].at[:, wide(blocks + i)]
        elif i < alone:
            target = out_refs[i]
        else:
            target = out_refs[alone].at[rows_of((i - alone) * tiles, tiles)]
        out_copies.append(
            pltpu.make_async_copy(out_buf.at[rows_of(i * tiles, tiles)], target, out_sem.at[i])
        )

    def one_block(i, _):
        first = i * tiles
        pl.when(i + 1 < blocks)(lambda: fetch_block(i + 1))
        rows = q_buf.at[rows_of(first, tiles)]
        pltpu.make_async_copy(rows, rows, q_sem.at[i]).wait()
        listed = kv_buf.at[rows_of(first * SLOTS, tiles * SLOTS)]
        pltpu.make_async_copy(listed, listed, kv_sem.at[i]).wait()
        early = tid_ref[first] + 1 < SLOTS

        @pl.when(early)
        def _():
            def one_tile(tile, _):
                attend_tiles(1, True, tile, tid_ref, q_buf, kv_buf, out_buf)
                return 0

            lax.fori_loop(first, first + tiles, one_tile, 0)

        @pl.when(jnp.logical_not(early))
        def _():
            count = 2 if tiles % 2 == 0 else 1

            def some_tiles(step, _):
                attend_tiles(count, False, first + step * count, tid_ref, q_buf, kv_buf, out_buf)
                return 0

            lax.fori_loop(0, tiles // count, some_tiles, 0)

        for k, copy in enumerate(out_copies):
            pl.when(i == k)(copy.start)
        return 0

    lax.fori_loop(0, blocks, one_block, 0)
    for copy_in, copy in zip(piece_ins, piece_outs):
        copy_in.wait()
        copy.start()
    for copy in piece_outs + out_copies:
        copy.wait()


def attend(turn, tiles, q_blocks, kv_bufs, loc, tid, out_at=None, shared=0, pieces=()):
    blocks, direct = len(q_blocks), out_at is not None
    queries = [q for q, _ in q_blocks]
    columns = [at for _, at in q_blocks] + list(out_at if direct else [])
    columns += [at for _, at in pieces]
    columns = jnp.stack([jnp.asarray(at, jnp.int32) for at in columns])
    starts, kv_tiles = [], 0
    for kv in kv_bufs:
        starts.append(kv_tiles)
        kv_tiles += kv.shape[0] // TILE
    smem = pl.BlockSpec(memory_space=pltpu.SMEM)
    hbm = pl.BlockSpec(memory_space=pl.ANY)
    units = blocks * tiles
    rows = tiles * TILE
    if direct:
        shapes = [(rows, HEADS * HEAD_DIM)]
    else:
        shapes = [(rows, WIDE)] * (blocks - shared) + [(shared * rows, WIDE)] * (shared > 0)
    out = pl.pallas_call(
        functools.partial(attend_kernel, blocks, tiles, starts, direct, shared, len(pieces)),
        out_shape=[jax.ShapeDtypeStruct(shape, jnp.bfloat16) for shape in shapes] + [jax.ShapeDtypeStruct((1,), jnp.int32)],
        in_specs=[smem] * 4 + [hbm] * (blocks + len(kv_bufs) + len(pieces)),
        out_specs=[hbm] * len(shapes) + [smem],
        scratch_shapes=[
            pltpu.VMEM((blocks * rows, WIDE), jnp.bfloat16),
            pltpu.VMEM((units * SLOTS * TILE, 2 * HEAD_DIM), jnp.bfloat16),
            pltpu.VMEM((blocks * rows, WIDE), jnp.bfloat16),
            pltpu.VMEM((max(len(pieces), 1) * rows, WIDE), jnp.bfloat16),
            pltpu.SemaphoreType.DMA((blocks,)),
            pltpu.SemaphoreType.DMA((blocks,)),
            pltpu.SemaphoreType.DMA((blocks + len(pieces),)),
            pltpu.SemaphoreType.DMA((max(len(pieces), 1),)),
        ],
        compiler_params=pltpu.CompilerParams(vmem_limit_bytes=VMEM_LIMIT),
        cost_estimate=pl.CostEstimate(flops=units * 10**10, bytes_accessed=10**6, transcendentals=0),
    )(turn, loc.reshape(-1), tid, columns, *queries, *kv_bufs, *[piece for piece, _ in pieces])
    return out


def deliver_kernel(sources, rows, col_ref, *refs):
    count, arrays = len(sources), len(refs) - 5
    out_ref, piece_buf, in_sem, out_sem = refs[arrays + 1:]
    ins = [
        pltpu.make_async_copy(refs[array].at[pl.ds(at * rows, rows)], piece_buf.at[i], in_sem.at[i])
        for i, (array, at) in enumerate(sources)
    ]
    outs = [
        pltpu.make_async_copy(
            piece_buf.at[i], out_ref.at[:, pl.ds(pl.multiple_of(col_ref[i], WIDE), WIDE)], out_sem.at[i]
        )
        for i in range(count)
    ]
    for copy in ins:
        copy.start()
    for copy_in, copy in zip(ins, outs):
        copy_in.wait()
        copy.start()
    for copy in outs:
        copy.wait()


def deliver(result, arrays, columns):
    rows = result.shape[0]
    sources = [(i, at) for i, array in enumerate(arrays) for at in range(array.shape[0] // rows)]
    count = len(sources)
    hbm = pl.BlockSpec(memory_space=pl.ANY)
    return pl.pallas_call(
        functools.partial(deliver_kernel, sources, rows),
        out_shape=jax.ShapeDtypeStruct(result.shape, result.dtype),
        in_specs=[pl.BlockSpec(memory_space=pltpu.SMEM)] + [hbm] * (len(arrays) + 1),
        out_specs=hbm,
        scratch_shapes=[
            pltpu.VMEM((count, rows, WIDE), jnp.bfloat16),
            pltpu.SemaphoreType.DMA((count,)),
            pltpu.SemaphoreType.DMA((count,)),
        ],
        input_output_aliases={len(arrays) + 1: 0},
        compiler_params=pltpu.CompilerParams(vmem_limit_bytes=VMEM_LIMIT),
    )(jnp.stack([jnp.asarray(at, jnp.int32) for at in columns]), *arrays, result)


def per_device(sizes, queries, key_rows, value_rows, tile_lists):
    kv_size, pb_size, z_size = sizes
    planes = kv_size * pb_size
    tokens = queries.shape[0]
    tiles = tokens // TILE
    z = lax.axis_index("head")
    b = lax.axis_index("kv") * pb_size + lax.axis_index("pb")
    core = b & 1

    def swap(x, offset):
        return lax.ppermute(x, AXES, [
            (i * z_size + h, (i ^ offset) * z_size + h) for i in range(planes) for h in range(z_size)
        ])

    def along(x, pairs):
        return lax.ppermute(x, AXES, [
            (i * z_size + h, i * z_size + k) for i in range(planes) for h, k in pairs
        ])

    relay = kv_size == 2 and pb_size == 4 and z_size == 4
    sides = (2, 4) if relay else (2, 2)
    halves = range(2)

    def head_of(half, offset):
        side = sides[half]
        mine = core + 2 * ((b & side) // side)
        return 4 * half + (mine ^ ((offset & 1) + 2 * ((offset & side) // side)))

    def near(half):
        return (0, 1, sides[half], sides[half] + 1)

    own_lists = lax.dynamic_slice_in_dim(tile_lists, z * tiles, tiles, axis=0)
    rider = jnp.concatenate([own_lists % 128, own_lists // 128], axis=0).astype(jnp.bfloat16)
    rider = jnp.pad(rider, ((0, -(2 * tiles) % 16), (0, 2 * HEAD_DIM - SLOTS)))
    own, lists = [], []
    for half in halves:
        blocks, riders = [], []
        for offset in near(half):
            at = head_of(half, offset) * HEAD_DIM
            piece = jnp.concatenate(
                [lax.dynamic_slice_in_dim(a, at, HEAD_DIM, axis=1) for a in (key_rows, value_rows)],
                axis=1,
            )
            piece = jnp.concatenate([piece, rider], axis=0)
            if offset:
                piece = swap(piece, offset)
            blocks.append(piece[:tokens])
            parts = piece[tokens:tokens + 2 * tiles, :SLOTS].astype(jnp.int32)
            riders.append(parts[:tiles] + 128 * parts[tiles:])
        own.append(jnp.concatenate(blocks, axis=0))
        lists.append(dict(zip(near(half), riders)))
    *own, queries = lax.optimization_barrier((*own, queries))

    def heads(array, at, count=1):
        return lax.dynamic_slice_in_dim(array, at, count * WIDE, axis=1)

    def query_pair(half):
        return heads(queries, (head_of(half, sides[half]) - core) * WIDE, 2)

    def tie(*arrays):
        return lax.optimization_barrier(arrays)

    def core_pairs(crossed):
        return jnp.concatenate([
            part for half in halves
            for part in (heads(queries, head_of(half, 1) * WIDE), heads(crossed[half], (1 - core) * WIDE))
        ], axis=1)

    if relay:
        across = [6 - side for side in sides]
        middle = jnp.logical_or(z == 1, z == 2)
        by_two, by_one = ((0, 2), (1, 3), (2, 0), (3, 1)), ((0, 1), (1, 0), (2, 3), (3, 2))
        outward, inward = ((1, 0), (2, 3)), ((1, 2), (2, 1))
        own_a, own_b = own
        rows = own_a.shape[0]
        both = jnp.concatenate(own, axis=0)
        two, one = along(both, by_two), along(both, by_one)
        own_a_far, own_b_far = swap(own_a, across[0]), swap(own_b, across[1])
        crossed_a = swap(query_pair(0), sides[0])
        turned_b, own_a_far = tie(query_pair(1), own_a_far)
        crossed_b = swap(turned_b, sides[1])
        both, one, two, own_a, own_b, own_a_far, own_b_far, crossed_a, crossed_b = tie(
            both, one, two, own_a, own_b, own_a_far, own_b_far, crossed_a, crossed_b
        )
        crossed = [crossed_a, crossed_b]
        outer, inner = along(two, outward), along(both, inward)
        pair_a = jnp.concatenate([one[:rows], two[:rows]], axis=0)
        pair_b = jnp.concatenate([one[rows:], two[rows:]], axis=0)
        pair_a_far, pair_b_far = swap(pair_a, across[0]), swap(pair_b, across[1])
        outer, inner, pair_a, pair_b, pair_a_far, pair_b_far, turned = tie(
            outer, inner, pair_a, pair_b, pair_a_far, pair_b_far, core_pairs(crossed)
        )
        by_core = swap(turned, 1)
        three = jnp.where(middle, inner, outer)
        three_a, three_b = three[:rows], three[rows:]
        kv_bufs = [
            [own_a, own_a_far, pair_a, pair_a_far, three_a, swap(three_a, across[0])],
            [own_b, own_b_far, pair_b, pair_b_far, three_b, swap(three_b, across[1])],
        ]
    else:
        kv_bufs = [[lax.all_gather(x, ("kv", "head"), axis=0, tiled=True)] for x in own]
        crossed = [swap(query_pair(half), sides[half]) for half in halves]
        by_core = swap(core_pairs(crossed), 1)

    def place(half, tile):
        device, within = tile // tiles, tile % tiles
        where, z_from = device // z_size, device % z_size
        differ = where ^ b
        side = sides[half]
        slot = (differ & 1) + 2 * ((differ & side) // side)
        if relay:
            distance, far = z_from ^ z, (differ & across[half]) // across[half]
            block = jnp.where(
                distance == 0, far, jnp.where(distance == 3, 6 + far, 1 + distance + 2 * far)
            )
        else:
            block = (where // pb_size) * z_size + z_from
        return (block * 4 + slot) * tiles + within

    kv_tiles = planes * z_size * tiles

    def operands(blocks):
        tids, locs, seen = [], [], []
        for half, offset in blocks:
            if half not in seen:
                seen.append(half)
            tids.append(((b ^ offset) * z_size + z) * tiles + jnp.arange(tiles, dtype=jnp.int32))
            locs.append(place(half, lists[half][offset]) + seen.index(half) * kv_tiles)
        q_blocks = []
        for half, offset in blocks:
            if offset == 0:
                q_blocks.append((queries, head_of(half, 0) * WIDE))
            elif offset == 1:
                q_blocks.append((by_core, 2 * half * WIDE))
            elif offset == sides[half]:
                q_blocks.append((crossed[half], core * WIDE))
            else:
                q_blocks.append((by_core, (2 * half + 1) * WIDE))
        bufs = [buf for half in seen for buf in kv_bufs[half]]
        return q_blocks, bufs, jnp.concatenate(locs, axis=0), jnp.concatenate(tids)

    diagonal = [(half, sides[half] + 1) for half in halves]
    straight, beside = [(half, sides[half]) for half in halves], [(half, 1) for half in halves]
    *outs, turn = attend(jnp.zeros((1,), jnp.int32), tiles, *operands(diagonal))
    *more, turn = attend(turn, tiles, *operands(straight + beside), shared=len(beside))
    sent = diagonal + straight + beside
    arrays = [swap(out, offset) for out, (_, offset) in zip(outs + more, sent)]
    columns = [head_of(half, offset) * WIDE for half, offset in sent]
    early = len(diagonal)
    result, _ = attend(
        turn, tiles, *operands([(half, 0) for half in halves]), [head_of(half, 0) * WIDE for half in halves],
        pieces=list(zip(arrays, columns))[:early],
    )
    return deliver(result, arrays[early:], columns[early:])


def solution(mesh):
    in_specs = (P(AXES, None), P(AXES, None), P(AXES, None), P(("kv", "pb"), None))
    sizes = tuple(mesh.shape[axis] for axis in AXES)
    return jax.shard_map(
        functools.partial(per_device, sizes),
        mesh=mesh, in_specs=in_specs, out_specs=P(AXES, None), check_vma=False,
    )
```

```python
import functools

import jax
import jax.numpy as jnp
from jax import lax
from jax.experimental import pallas as pl
from jax.experimental.pallas import tpu as pltpu
from jax.sharding import PartitionSpec as P

HEADS = 64
KV_HEADS = 8
HEAD_DIM = 128
TILE = 128
SLOTS = 8

NEG = -1e30
GROUPS = HEADS // KV_HEADS
WIDE = GROUPS * HEAD_DIM
VMEM_LIMIT, DELIVER_LIMIT = 60 * 2**20, 8 * 2**20
AXES = ("kv", "pb", "head")
LOG2 = HEAD_DIM ** (-0.5) * 1.4426950408889634


def rows_of(tile, count=1):
    return pl.ds(pl.multiple_of(tile * TILE, TILE), count * TILE)


def attend_tiles(count, masked, first, tid_ref, q_buf, kv_buf, out_buf):
    keys, values = [], []
    for t in range(count):
        listed = rows_of((first + t) * SLOTS, SLOTS)
        keys.append(kv_buf[listed, :HEAD_DIM])
        value = kv_buf[listed, HEAD_DIM:]
        values.append(jnp.concatenate([value, jnp.ones_like(value)], axis=1))
    row = lax.broadcasted_iota(jnp.int32, (TILE, TILE), 0)
    column = lax.broadcasted_iota(jnp.int32, (TILE, TILE), 1)
    diagonal = jnp.where(column <= row, 0.0, NEG)

    def score(t, g):
        scores = lax.dot_general(
            q_buf[rows_of(first + t), g * HEAD_DIM:(g + 1) * HEAD_DIM], keys[t], (((1,), (1,)), ((), ())),
            preferred_element_type=jnp.float32,
        )
        parts = [scores[:, :TILE] + diagonal]
        if masked:
            live = tid_ref[first + t] + 1
            for j in range(1, SLOTS):
                part = scores[:, j * TILE:(j + 1) * TILE]
                parts.append(part + jnp.where(j < live, 0.0, NEG))
        else:
            parts.append(scores[:, TILE:])
        return jnp.concatenate(parts, axis=1)

    def weigh(scores):
        top = jnp.max(scores, axis=1, keepdims=True)
        return jnp.exp2((scores - top) * LOG2).astype(jnp.bfloat16)

    def finish(weights, t, g):
        total = jnp.dot(weights, values[t], preferred_element_type=jnp.float32)
        out = total[:, :HEAD_DIM] / total[:, HEAD_DIM:]
        out_buf[rows_of(first + t), g * HEAD_DIM:(g + 1) * HEAD_DIM] = out.astype(jnp.bfloat16)

    units = [(t, g) for t in range(count) for g in range(GROUPS)]
    ahead = 0 if masked else 3
    scores, weights = {}, {}
    for step in range(len(units) + ahead + 1):
        if step < len(units):
            scores[step] = score(*units[step])
        if 0 <= step - ahead < len(units):
            weights[step - ahead] = weigh(scores.pop(step - ahead))
        if step - ahead >= 1:
            finish(weights.pop(step - ahead - 1), *units[step - ahead - 1])


def attend_kernel(blocks, tiles, starts, direct, shared, pieces, turn_ref, loc_ref, tid_ref, col_ref, *refs):
    q_refs, refs = refs[:blocks], refs[blocks:]
    kv_refs, refs = refs[:len(starts)], refs[len(starts):]
    piece_refs, refs = refs[:pieces], refs[pieces:]
    out_refs, (next_ref, q_buf, kv_buf, out_buf, piece_buf, *sems) = refs[:-9], refs[-9:]
    q_sem, kv_sem, out_sem, piece_sem = sems
    next_ref[0] = turn_ref[0] + 1

    def wide(i):
        return pl.ds(pl.multiple_of(col_ref[i], WIDE), WIDE)

    q_copies = [
        pltpu.make_async_copy(
            q_refs[i].at[:, wide(i)], q_buf.at[rows_of(i * tiles, tiles)], q_sem.at[i]
        )
        for i in range(blocks)
    ]

    def fetch_from(first, last, at, slot, sem):
        if last - first == 1:
            source = kv_refs[first].at[rows_of(at - starts[first])]
            pltpu.make_async_copy(source, kv_buf.at[rows_of(slot)], sem).start()
            return 0
        cut = (first + last) // 2
        return lax.cond(
            at < starts[cut],
            lambda: fetch_from(first, cut, at, slot, sem),
            lambda: fetch_from(cut, last, at, slot, sem),
        )

    def fetch_block(i):
        slots = tiles * SLOTS
        for k, copy in enumerate(q_copies):
            pl.when(i == k)(copy.start)

        def one_slot(slot, _):
            return fetch_from(0, len(kv_refs), loc_ref[slot], slot, kv_sem.at[i])

        return lax.fori_loop(i * slots, (i + 1) * slots, one_slot, 0)

    lax.fori_loop(0, blocks, lambda i, _: fetch_block(i), 0)
    piece_ins, piece_outs = [], []
    for i in range(pieces):
        buf = piece_buf.at[rows_of(i * tiles, tiles)]
        piece_ins.append(pltpu.make_async_copy(piece_refs[i], buf, piece_sem.at[i]))
        piece_outs.append(
            pltpu.make_async_copy(buf, out_refs[0].at[:, wide(2 * blocks + i)], out_sem.at[blocks + i])
        )
        piece_ins[-1].start()

    out_copies = []
    for i in range(blocks):
        alone = blocks - shared
        if direct:
            target = out_refs[0].at[:, wide(blocks + i)]
        elif i < alone:
            target = out_refs[i]
        else:
            target = out_refs[alone].at[rows_of((i - alone) * tiles, tiles)]
        out_copies.append(
            pltpu.make_async_copy(out_buf.at[rows_of(i * tiles, tiles)], target, out_sem.at[i])
        )

    def one_block(i, _):
        first = i * tiles
        rows = q_buf.at[rows_of(first, tiles)]
        pltpu.make_async_copy(rows, rows, q_sem.at[i]).wait()
        listed = kv_buf.at[rows_of(first * SLOTS, tiles * SLOTS)]
        pltpu.make_async_copy(listed, listed, kv_sem.at[i]).wait()
        early = tid_ref[first] + 1 < SLOTS

        @pl.when(early)
        def _():
            def one_tile(tile, _):
                attend_tiles(1, True, tile, tid_ref, q_buf, kv_buf, out_buf)
                return 0

            lax.fori_loop(first, first + tiles, one_tile, 0)

        @pl.when(jnp.logical_not(early))
        def _():
            count = 2 if tiles % 2 == 0 else 1

            def some_tiles(step, _):
                attend_tiles(count, False, first + step * count, tid_ref, q_buf, kv_buf, out_buf)
                return 0

            lax.fori_loop(0, tiles // count, some_tiles, 0)

        for k, copy in enumerate(out_copies):
            pl.when(i == k)(copy.start)
        return 0

    lax.fori_loop(0, blocks, one_block, 0)
    for copy_in, copy in zip(piece_ins, piece_outs):
        copy_in.wait()
        copy.start()
    for copy in piece_outs + out_copies:
        copy.wait()


def attend(turn, tiles, q_blocks, kv_bufs, loc, tid, out_at=None, shared=0, pieces=()):
    blocks, direct = len(q_blocks), out_at is not None
    queries = [q for q, _ in q_blocks]
    columns = [at for _, at in q_blocks] + list(out_at if direct else [])
    columns += [at for _, at in pieces]
    columns = jnp.stack([jnp.asarray(at, jnp.int32) for at in columns])
    starts, kv_tiles = [], 0
    for kv in kv_bufs:
        starts.append(kv_tiles)
        kv_tiles += kv.shape[0] // TILE
    smem = pl.BlockSpec(memory_space=pltpu.SMEM)
    hbm = pl.BlockSpec(memory_space=pl.ANY)
    units = blocks * tiles
    rows = tiles * TILE
    if direct:
        shapes = [(rows, HEADS * HEAD_DIM)]
    else:
        shapes = [(rows, WIDE)] * (blocks - shared) + [(shared * rows, WIDE)] * (shared > 0)
    out = pl.pallas_call(
        functools.partial(attend_kernel, blocks, tiles, starts, direct, shared, len(pieces)),
        out_shape=[jax.ShapeDtypeStruct(shape, jnp.bfloat16) for shape in shapes] + [jax.ShapeDtypeStruct((1,), jnp.int32)],
        in_specs=[smem] * 4 + [hbm] * (blocks + len(kv_bufs) + len(pieces)),
        out_specs=[hbm] * len(shapes) + [smem],
        scratch_shapes=[
            pltpu.VMEM((blocks * rows, WIDE), jnp.bfloat16),
            pltpu.VMEM((units * SLOTS * TILE, 2 * HEAD_DIM), jnp.bfloat16),
            pltpu.VMEM((blocks * rows, WIDE), jnp.bfloat16),
            pltpu.VMEM((max(len(pieces), 1) * rows, WIDE), jnp.bfloat16),
            pltpu.SemaphoreType.DMA((blocks,)),
            pltpu.SemaphoreType.DMA((blocks,)),
            pltpu.SemaphoreType.DMA((blocks + len(pieces),)),
            pltpu.SemaphoreType.DMA((max(len(pieces), 1),)),
        ],
        compiler_params=pltpu.CompilerParams(vmem_limit_bytes=VMEM_LIMIT),
        cost_estimate=pl.CostEstimate(flops=units * 10**10, bytes_accessed=10**6, transcendentals=0),
    )(turn, loc.reshape(-1), tid, columns, *queries, *kv_bufs, *[piece for piece, _ in pieces])
    return out


def deliver_kernel(sources, rows, col_ref, *refs):
    out_ref, sem = refs[-2:]
    copies = [
        pltpu.make_async_copy(
            refs[array].at[pl.ds(at * rows, rows)],
            out_ref.at[:, pl.ds(pl.multiple_of(col_ref[i], WIDE), WIDE)], sem.at[i],
        )
        for i, (array, at) in enumerate(sources)
    ]
    for copy in copies:
        copy.start()
    for copy in copies:
        copy.wait()


def deliver(result, arrays, columns):
    rows = result.shape[0]
    sources = [(i, at) for i, array in enumerate(arrays) for at in range(array.shape[0] // rows)]
    hbm = pl.BlockSpec(memory_space=pl.ANY)
    return pl.pallas_call(
        functools.partial(deliver_kernel, sources, rows),
        out_shape=jax.ShapeDtypeStruct(result.shape, result.dtype),
        in_specs=[pl.BlockSpec(memory_space=pltpu.SMEM)]
        + [pl.BlockSpec(memory_space=pltpu.VMEM)] * len(arrays) + [hbm],
        out_specs=hbm,
        scratch_shapes=[pltpu.SemaphoreType.DMA((len(sources),))],
        input_output_aliases={len(arrays) + 1: 0},
        compiler_params=pltpu.CompilerParams(vmem_limit_bytes=DELIVER_LIMIT),
    )(jnp.stack([jnp.asarray(at, jnp.int32) for at in columns]), *arrays, result)


def per_device(sizes, queries, key_rows, value_rows, tile_lists):
    kv_size, pb_size, z_size = sizes
    planes = kv_size * pb_size
    tokens = queries.shape[0]
    tiles = tokens // TILE
    z = lax.axis_index("head")
    b = lax.axis_index("kv") * pb_size + lax.axis_index("pb")
    core = b & 1

    def swap(x, offset):
        return lax.ppermute(x, AXES, [
            (i * z_size + h, (i ^ offset) * z_size + h) for i in range(planes) for h in range(z_size)
        ])

    def along(x, pairs):
        return lax.ppermute(x, AXES, [
            (i * z_size + h, i * z_size + k) for i in range(planes) for h, k in pairs
        ])

    relay = kv_size == 2 and pb_size == 4 and z_size == 4
    sides = (2, 4) if relay else (2, 2)
    halves = range(2)

    def head_of(half, offset):
        side = sides[half]
        mine = core + 2 * ((b & side) // side)
        return 4 * half + (mine ^ ((offset & 1) + 2 * ((offset & side) // side)))

    def near(half):
        return (0, 1, sides[half], sides[half] + 1)

    own_lists = lax.dynamic_slice_in_dim(tile_lists, z * tiles, tiles, axis=0)
    rider = jnp.concatenate([own_lists % 128, own_lists // 128], axis=0).astype(jnp.bfloat16)
    rider = jnp.pad(rider, ((0, -(2 * tiles) % 16), (0, 2 * HEAD_DIM - SLOTS)))

    def key_block(half, offset):
        at = head_of(half, offset) * HEAD_DIM
        return jnp.concatenate(
            [lax.dynamic_slice_in_dim(a, at, HEAD_DIM, axis=1) for a in (key_rows, value_rows)], axis=1
        )

    blocks = {(half, 0): key_block(half, 0) for half in halves}
    riders = {0: rider}
    for group in [[(0, 1), (1, 1)]] + [[(half, sides[half] + c)] for half in halves for c in (0, 1)]:
        offset = group[0][1]
        came = swap(jnp.concatenate([key_block(*block) for block in group] + [rider], axis=0), offset)
        for i, block in enumerate(group):
            blocks[block] = came[i * tokens:(i + 1) * tokens]
        riders[offset] = came[len(group) * tokens:]
    own = [jnp.concatenate([blocks[half, offset] for offset in near(half)], axis=0) for half in halves]
    lists = {}
    for offset, came in riders.items():
        parts = came[:2 * tiles, :SLOTS].astype(jnp.int32)
        lists[offset] = parts[:tiles] + 128 * parts[tiles:]
    *own, queries = lax.optimization_barrier((*own, queries))

    def heads(array, at, count=1):
        return lax.dynamic_slice_in_dim(array, at, count * WIDE, axis=1)

    def query_pair(half):
        return heads(queries, (head_of(half, sides[half]) - core) * WIDE, 2)

    def tie(*arrays):
        return lax.optimization_barrier(arrays)

    def core_pairs(crossed):
        return jnp.concatenate([
            part for half in halves
            for part in (heads(queries, head_of(half, 1) * WIDE), heads(crossed[half], (1 - core) * WIDE))
        ], axis=1)

    if relay:
        across = [6 - side for side in sides]
        middle = jnp.logical_or(z == 1, z == 2)
        by_two, by_one = ((0, 2), (1, 3), (2, 0), (3, 1)), ((0, 1), (1, 0), (2, 3), (3, 2))
        outward, inward = ((1, 0), (2, 3)), ((1, 2), (2, 1))
        own_a, own_b = own
        rows = own_a.shape[0]
        both = jnp.concatenate(own, axis=0)
        two, one = along(both, by_two), along(both, by_one)
        own_a_far, own_b_far = swap(own_a, across[0]), swap(own_b, across[1])
        crossed_a = swap(query_pair(0), sides[0])
        turned_b, own_a_far = tie(query_pair(1), own_a_far)
        crossed_b = swap(turned_b, sides[1])
        both, one, two, own_a, own_b, own_a_far, own_b_far, crossed_a, crossed_b = tie(
            both, one, two, own_a, own_b, own_a_far, own_b_far, crossed_a, crossed_b
        )
        crossed = [crossed_a, crossed_b]
        outer, inner = along(two, outward), along(both, inward)
        pair_a = jnp.concatenate([one[:rows], two[:rows]], axis=0)
        pair_b = jnp.concatenate([one[rows:], two[rows:]], axis=0)
        pair_a_far, pair_b_far = swap(pair_a, across[0]), swap(pair_b, across[1])
        outer, inner, pair_a, pair_b, pair_a_far, pair_b_far, turned = tie(
            outer, inner, pair_a, pair_b, pair_a_far, pair_b_far, core_pairs(crossed)
        )
        by_core = swap(turned, 1)
        three = jnp.where(middle, inner, outer)
        three_a, three_b = three[:rows], three[rows:]
        kv_bufs = [
            [own_a, own_a_far, pair_a, pair_a_far, three_a, swap(three_a, across[0])],
            [own_b, own_b_far, pair_b, pair_b_far, three_b, swap(three_b, across[1])],
        ]
    else:
        kv_bufs = [[lax.all_gather(x, ("kv", "head"), axis=0, tiled=True)] for x in own]
        crossed = [swap(query_pair(half), sides[half]) for half in halves]
        by_core = swap(core_pairs(crossed), 1)

    def place(half, tile):
        device, within = tile // tiles, tile % tiles
        where, z_from = device // z_size, device % z_size
        differ = where ^ b
        side = sides[half]
        slot = (differ & 1) + 2 * ((differ & side) // side)
        if relay:
            distance, far = z_from ^ z, (differ & across[half]) // across[half]
            block = jnp.where(
                distance == 0, far, jnp.where(distance == 3, 6 + far, 1 + distance + 2 * far)
            )
        else:
            block = (where // pb_size) * z_size + z_from
        return (block * 4 + slot) * tiles + within

    kv_tiles = planes * z_size * tiles

    def operands(blocks):
        tids, locs, seen = [], [], []
        for half, offset in blocks:
            if half not in seen:
                seen.append(half)
            tids.append(((b ^ offset) * z_size + z) * tiles + jnp.arange(tiles, dtype=jnp.int32))
            locs.append(place(half, lists[offset]) + seen.index(half) * kv_tiles)
        q_blocks = []
        for half, offset in blocks:
            if offset == 0:
                q_blocks.append((queries, head_of(half, 0) * WIDE))
            elif offset == 1:
                q_blocks.append((by_core, 2 * half * WIDE))
            elif offset == sides[half]:
                q_blocks.append((crossed[half], core * WIDE))
            else:
                q_blocks.append((by_core, (2 * half + 1) * WIDE))
        bufs = [buf for half in seen for buf in kv_bufs[half]]
        return q_blocks, bufs, jnp.concatenate(locs, axis=0), jnp.concatenate(tids)

    diagonal = [(half, sides[half] + 1) for half in halves]
    straight, beside = [(half, sides[half]) for half in halves], [(half, 1) for half in halves]
    *outs, turn = attend(jnp.zeros((1,), jnp.int32), tiles, *operands(diagonal))
    *more, turn = attend(turn, tiles, *operands(straight + beside), shared=len(beside))
    sent = diagonal + straight + beside
    arrays = [swap(out, offset) for out, (_, offset) in zip(outs + more, sent)]
    columns = [head_of(half, offset) * WIDE for half, offset in sent]
    early = len(diagonal)
    result, _ = attend(
        turn, tiles, *operands([(half, 0) for half in halves]), [head_of(half, 0) * WIDE for half in halves],
        pieces=list(zip(arrays, columns))[:early],
    )
    return deliver(result, arrays[early:], columns[early:])


def solution(mesh):
    in_specs = (P(AXES, None), P(AXES, None), P(AXES, None), P(("kv", "pb"), None))
    sizes = tuple(mesh.shape[axis] for axis in AXES)
    return jax.shard_map(
        functools.partial(per_device, sizes),
        mesh=mesh, in_specs=in_specs, out_specs=P(AXES, None), check_vma=False,
    )
```

```python
import functools

import jax
import jax.numpy as jnp
from jax import lax
from jax.experimental import pallas as pl
from jax.experimental.pallas import tpu as pltpu
from jax.sharding import PartitionSpec as P

HEADS = 64
KV_HEADS = 8
HEAD_DIM = 128
TILE = 128
SLOTS = 8

NEG = -1e30
GROUPS = HEADS // KV_HEADS
WIDE = GROUPS * HEAD_DIM
VMEM_LIMIT, DELIVER_LIMIT = 60 * 2**20, 8 * 2**20
AXES = ("kv", "pb", "head")
LOG2 = HEAD_DIM ** (-0.5) * 1.4426950408889634


def rows_of(tile, count=1):
    return pl.ds(pl.multiple_of(tile * TILE, TILE), count * TILE)


def attend_tiles(count, masked, first, tid_ref, q_buf, kv_buf, out_buf):
    keys, values = [], []
    for t in range(count):
        listed = rows_of((first + t) * SLOTS, SLOTS)
        keys.append(kv_buf[listed, :HEAD_DIM])
        value = kv_buf[listed, HEAD_DIM:]
        values.append(jnp.concatenate([value, jnp.ones_like(value)], axis=1))
    row = lax.broadcasted_iota(jnp.int32, (TILE, TILE), 0)
    column = lax.broadcasted_iota(jnp.int32, (TILE, TILE), 1)
    diagonal = jnp.where(column <= row, 0.0, NEG)

    def score(t, g):
        scores = lax.dot_general(
            q_buf[rows_of(first + t), g * HEAD_DIM:(g + 1) * HEAD_DIM], keys[t], (((1,), (1,)), ((), ())),
            preferred_element_type=jnp.float32,
        )
        parts = [scores[:, :TILE] + diagonal]
        if masked:
            live = tid_ref[first + t] + 1
            for j in range(1, SLOTS):
                part = scores[:, j * TILE:(j + 1) * TILE]
                parts.append(part + jnp.where(j < live, 0.0, NEG))
        else:
            parts.append(scores[:, TILE:])
        return jnp.concatenate(parts, axis=1)

    def weigh(scores):
        top = jnp.max(scores, axis=1, keepdims=True)
        return jnp.exp2((scores - top) * LOG2).astype(jnp.bfloat16)

    def finish(weights, t, g):
        total = jnp.dot(weights, values[t], preferred_element_type=jnp.float32)
        out = total[:, :HEAD_DIM] / total[:, HEAD_DIM:]
        out_buf[rows_of(first + t), g * HEAD_DIM:(g + 1) * HEAD_DIM] = out.astype(jnp.bfloat16)

    units = [(t, g) for t in range(count) for g in range(GROUPS)]
    ahead = 0 if masked else 3
    scores, weights = {}, {}
    for step in range(len(units) + ahead + 1):
        if step < len(units):
            scores[step] = score(*units[step])
        if 0 <= step - ahead < len(units):
            weights[step - ahead] = weigh(scores.pop(step - ahead))
        if step - ahead >= 1:
            finish(weights.pop(step - ahead - 1), *units[step - ahead - 1])


def attend_kernel(blocks, tiles, starts, direct, shared, pieces, turn_ref, loc_ref, tid_ref, col_ref, *refs):
    q_refs, refs = refs[:blocks], refs[blocks:]
    kv_refs, refs = refs[:len(starts)], refs[len(starts):]
    piece_refs, refs = refs[:pieces], refs[pieces:]
    out_refs, (next_ref, q_buf, kv_buf, out_buf, piece_buf, *sems) = refs[:-9], refs[-9:]
    q_sem, kv_sem, out_sem, piece_sem = sems
    next_ref[0] = turn_ref[0] + 1

    def wide(i):
        return pl.ds(pl.multiple_of(col_ref[i], WIDE), WIDE)

    q_copies = [
        pltpu.make_async_copy(
            q_refs[i].at[:, wide(i)], q_buf.at[rows_of(i * tiles, tiles)], q_sem.at[i]
        )
        for i in range(blocks)
    ]

    def fetch_from(first, last, at, slot, sem):
        if last - first == 1:
            source = kv_refs[first].at[rows_of(at - starts[first])]
            pltpu.make_async_copy(source, kv_buf.at[rows_of(slot)], sem).start()
            return 0
        cut = (first + last) // 2
        return lax.cond(
            at < starts[cut],
            lambda: fetch_from(first, cut, at, slot, sem),
            lambda: fetch_from(cut, last, at, slot, sem),
        )

    def fetch_block(i):
        slots = tiles * SLOTS
        for k, copy in enumerate(q_copies):
            pl.when(i == k)(copy.start)

        def one_slot(slot, _):
            return fetch_from(0, len(kv_refs), loc_ref[slot], slot, kv_sem.at[i])

        return lax.fori_loop(i * slots, (i + 1) * slots, one_slot, 0)

    lax.fori_loop(0, blocks, lambda i, _: fetch_block(i), 0)
    piece_ins, piece_outs = [], []
    for i in range(pieces):
        buf = piece_buf.at[rows_of(i * tiles, tiles)]
        piece_ins.append(pltpu.make_async_copy(piece_refs[i], buf, piece_sem.at[i]))
        piece_outs.append(
            pltpu.make_async_copy(buf, out_refs[0].at[:, wide(2 * blocks + i)], out_sem.at[blocks + i])
        )
        piece_ins[-1].start()

    out_copies = []
    for i in range(blocks):
        alone = blocks - shared
        if direct:
            target = out_refs[0].at[:, wide(blocks + i)]
        elif i < alone:
            target = out_refs[i]
        else:
            target = out_refs[alone].at[rows_of((i - alone) * tiles, tiles)]
        out_copies.append(
            pltpu.make_async_copy(out_buf.at[rows_of(i * tiles, tiles)], target, out_sem.at[i])
        )

    def one_block(i, _):
        first = i * tiles
        rows = q_buf.at[rows_of(first, tiles)]
        pltpu.make_async_copy(rows, rows, q_sem.at[i]).wait()
        listed = kv_buf.at[rows_of(first * SLOTS, tiles * SLOTS)]
        pltpu.make_async_copy(listed, listed, kv_sem.at[i]).wait()
        early = tid_ref[first] + 1 < SLOTS

        @pl.when(early)
        def _():
            def one_tile(tile, _):
                attend_tiles(1, True, tile, tid_ref, q_buf, kv_buf, out_buf)
                return 0

            lax.fori_loop(first, first + tiles, one_tile, 0)

        @pl.when(jnp.logical_not(early))
        def _():
            count = 2 if tiles % 2 == 0 else 1

            def some_tiles(step, _):
                attend_tiles(count, False, first + step * count, tid_ref, q_buf, kv_buf, out_buf)
                return 0

            lax.fori_loop(0, tiles // count, some_tiles, 0)

        for k, copy in enumerate(out_copies):
            pl.when(i == k)(copy.start)
        return 0

    lax.fori_loop(0, blocks, one_block, 0)
    for copy_in, copy in zip(piece_ins, piece_outs):
        copy_in.wait()
        copy.start()
    for copy in piece_outs + out_copies:
        copy.wait()


def attend(turn, tiles, q_blocks, kv_bufs, loc, tid, out_at=None, shared=0, pieces=()):
    blocks, direct = len(q_blocks), out_at is not None
    queries = [q for q, _ in q_blocks]
    columns = [at for _, at in q_blocks] + list(out_at if direct else [])
    columns += [at for _, at in pieces]
    columns = jnp.stack([jnp.asarray(at, jnp.int32) for at in columns])
    starts, kv_tiles = [], 0
    for kv in kv_bufs:
        starts.append(kv_tiles)
        kv_tiles += kv.shape[0] // TILE
    smem = pl.BlockSpec(memory_space=pltpu.SMEM)
    hbm = pl.BlockSpec(memory_space=pl.ANY)
    units = blocks * tiles
    rows = tiles * TILE
    if direct:
        shapes = [(rows, HEADS * HEAD_DIM)]
    else:
        shapes = [(rows, WIDE)] * (blocks - shared) + [(shared * rows, WIDE)] * (shared > 0)
    out = pl.pallas_call(
        functools.partial(attend_kernel, blocks, tiles, starts, direct, shared, len(pieces)),
        out_shape=[jax.ShapeDtypeStruct(shape, jnp.bfloat16) for shape in shapes] + [jax.ShapeDtypeStruct((1,), jnp.int32)],
        in_specs=[smem] * 4 + [hbm] * (blocks + len(kv_bufs) + len(pieces)),
        out_specs=[hbm] * len(shapes) + [smem],
        scratch_shapes=[
            pltpu.VMEM((blocks * rows, WIDE), jnp.bfloat16),
            pltpu.VMEM((units * SLOTS * TILE, 2 * HEAD_DIM), jnp.bfloat16),
            pltpu.VMEM((blocks * rows, WIDE), jnp.bfloat16),
            pltpu.VMEM((max(len(pieces), 1) * rows, WIDE), jnp.bfloat16),
            pltpu.SemaphoreType.DMA((blocks,)),
            pltpu.SemaphoreType.DMA((blocks,)),
            pltpu.SemaphoreType.DMA((blocks + len(pieces),)),
            pltpu.SemaphoreType.DMA((max(len(pieces), 1),)),
        ],
        compiler_params=pltpu.CompilerParams(vmem_limit_bytes=VMEM_LIMIT),
        cost_estimate=pl.CostEstimate(flops=units * 10**10, bytes_accessed=10**6, transcendentals=0),
    )(turn, loc.reshape(-1), tid, columns, *queries, *kv_bufs, *[piece for piece, _ in pieces])
    return out


def deliver_kernel(sources, rows, col_ref, *refs):
    out_ref, sem = refs[-2:]
    copies = [
        pltpu.make_async_copy(
            refs[array].at[pl.ds(at * rows, rows)],
            out_ref.at[:, pl.ds(pl.multiple_of(col_ref[i], WIDE), WIDE)], sem.at[i],
        )
        for i, (array, at) in enumerate(sources)
    ]
    for copy in copies:
        copy.start()
    for copy in copies:
        copy.wait()


def deliver(result, arrays, columns):
    rows = result.shape[0]
    sources = [(i, at) for i, array in enumerate(arrays) for at in range(array.shape[0] // rows)]
    hbm = pl.BlockSpec(memory_space=pl.ANY)
    return pl.pallas_call(
        functools.partial(deliver_kernel, sources, rows),
        out_shape=jax.ShapeDtypeStruct(result.shape, result.dtype),
        in_specs=[pl.BlockSpec(memory_space=pltpu.SMEM)]
        + [pl.BlockSpec(memory_space=pltpu.VMEM)] * len(arrays) + [hbm],
        out_specs=hbm,
        scratch_shapes=[pltpu.SemaphoreType.DMA((len(sources),))],
        input_output_aliases={len(arrays) + 1: 0},
        compiler_params=pltpu.CompilerParams(vmem_limit_bytes=DELIVER_LIMIT),
    )(jnp.stack([jnp.asarray(at, jnp.int32) for at in columns]), *arrays, result)


def per_device(sizes, queries, key_rows, value_rows, tile_lists):
    kv_size, pb_size, z_size = sizes
    planes = kv_size * pb_size
    tokens = queries.shape[0]
    tiles = tokens // TILE
    z = lax.axis_index("head")
    b = lax.axis_index("kv") * pb_size + lax.axis_index("pb")
    core = b & 1

    def swap(x, offset):
        return lax.ppermute(x, AXES, [
            (i * z_size + h, (i ^ offset) * z_size + h) for i in range(planes) for h in range(z_size)
        ])

    def along(x, pairs):
        return lax.ppermute(x, AXES, [
            (i * z_size + h, i * z_size + k) for i in range(planes) for h, k in pairs
        ])

    relay = kv_size == 2 and pb_size == 4 and z_size == 4
    sides = (2, 4) if relay else (2, 2)
    halves = range(2)

    def head_of(half, offset):
        side = sides[half]
        mine = core + 2 * ((b & side) // side)
        return 4 * half + (mine ^ ((offset & 1) + 2 * ((offset & side) // side)))

    def near(half):
        return (0, 1, sides[half], sides[half] + 1)

    own_lists = lax.dynamic_slice_in_dim(tile_lists, z * tiles, tiles, axis=0)
    rider = jnp.concatenate([own_lists % 128, own_lists // 128], axis=0).astype(jnp.bfloat16)
    rider = jnp.pad(rider, ((0, -(2 * tiles) % 16), (0, 2 * HEAD_DIM - SLOTS)))

    def key_block(half, offset):
        at = head_of(half, offset) * HEAD_DIM
        return jnp.concatenate(
            [lax.dynamic_slice_in_dim(a, at, HEAD_DIM, axis=1) for a in (key_rows, value_rows)], axis=1
        )

    blocks = {(half, 0): key_block(half, 0) for half in halves}
    riders = {0: rider}
    for group in [[(0, 1), (1, 1)]] + [[(half, sides[half] + c)] for half in halves for c in (0, 1)]:
        offset = group[0][1]
        came = swap(jnp.concatenate([key_block(*block) for block in group] + [rider], axis=0), offset)
        for i, block in enumerate(group):
            blocks[block] = came[i * tokens:(i + 1) * tokens]
        riders[offset] = came[len(group) * tokens:]
    own = [jnp.concatenate([blocks[half, offset] for offset in near(half)], axis=0) for half in halves]
    lists = {}
    for offset, came in riders.items():
        parts = came[:2 * tiles, :SLOTS].astype(jnp.int32)
        lists[offset] = parts[:tiles] + 128 * parts[tiles:]
    *own, queries = lax.optimization_barrier((*own, queries))

    def heads(array, at, count=1):
        return lax.dynamic_slice_in_dim(array, at, count * WIDE, axis=1)

    def query_pair(half):
        return heads(queries, (head_of(half, sides[half]) - core) * WIDE, 2)

    def tie(*arrays):
        return lax.optimization_barrier(arrays)

    def core_pairs(crossed):
        return jnp.concatenate([
            part for half in halves
            for part in (heads(queries, head_of(half, 1) * WIDE), heads(crossed[half], (1 - core) * WIDE))
        ], axis=1)

    if relay:
        across = [6 - side for side in sides]
        middle = jnp.logical_or(z == 1, z == 2)
        by_two, by_one = ((0, 2), (1, 3), (2, 0), (3, 1)), ((0, 1), (1, 0), (2, 3), (3, 2))
        outward, inward = ((1, 0), (2, 3)), ((1, 2), (2, 1))
        own_a, own_b = own
        rows = own_a.shape[0]
        both = jnp.concatenate(own, axis=0)
        two, one = along(both, by_two), along(both, by_one)
        own_a_far, own_b_far = swap(own_a, across[0]), swap(own_b, across[1])
        crossed_a = swap(query_pair(0), sides[0])
        turned_b, own_a_far = tie(query_pair(1), own_a_far)
        crossed_b = swap(turned_b, sides[1])
        both, one, two, own_a, own_b, own_a_far, own_b_far, crossed_a, crossed_b = tie(
            both, one, two, own_a, own_b, own_a_far, own_b_far, crossed_a, crossed_b
        )
        crossed = [crossed_a, crossed_b]
        outer, inner = along(two, outward), along(both, inward)
        pair_a = jnp.concatenate([one[:rows], two[:rows]], axis=0)
        pair_b = jnp.concatenate([one[rows:], two[rows:]], axis=0)
        pair_a_far, pair_b_far = swap(pair_a, across[0]), swap(pair_b, across[1])
        outer, inner, pair_a, pair_b, pair_a_far, pair_b_far, turned = tie(
            outer, inner, pair_a, pair_b, pair_a_far, pair_b_far, core_pairs(crossed)
        )
        by_core = swap(turned, 1)
        three = jnp.where(middle, inner, outer)
        three_a, three_b = three[:rows], three[rows:]
        kv_bufs = [
            [own_a, own_a_far, pair_a, pair_a_far, three_a, swap(three_a, across[0])],
            [own_b, own_b_far, pair_b, pair_b_far, three_b, swap(three_b, across[1])],
        ]
    else:
        kv_bufs = [[lax.all_gather(x, ("kv", "head"), axis=0, tiled=True)] for x in own]
        crossed = [swap(query_pair(half), sides[half]) for half in halves]
        by_core = swap(core_pairs(crossed), 1)

    def place(half, tile):
        device, within = tile // tiles, tile % tiles
        where, z_from = device // z_size, device % z_size
        differ = where ^ b
        side = sides[half]
        slot = (differ & 1) + 2 * ((differ & side) // side)
        if relay:
            distance, far = z_from ^ z, (differ & across[half]) // across[half]
            block = jnp.where(
                distance == 0, far, jnp.where(distance == 3, 6 + far, 1 + distance + 2 * far)
            )
        else:
            block = (where // pb_size) * z_size + z_from
        return (block * 4 + slot) * tiles + within

    kv_tiles = planes * z_size * tiles

    def operands(blocks):
        tids, locs, seen = [], [], []
        for half, offset in blocks:
            if half not in seen:
                seen.append(half)
            tids.append(((b ^ offset) * z_size + z) * tiles + jnp.arange(tiles, dtype=jnp.int32))
            locs.append(place(half, lists[offset]) + seen.index(half) * kv_tiles)
        q_blocks = []
        for half, offset in blocks:
            if offset == 0:
                q_blocks.append((queries, head_of(half, 0) * WIDE))
            elif offset == 1:
                q_blocks.append((by_core, 2 * half * WIDE))
            elif offset == sides[half]:
                q_blocks.append((crossed[half], core * WIDE))
            else:
                q_blocks.append((by_core, (2 * half + 1) * WIDE))
        bufs = [buf for half in seen for buf in kv_bufs[half]]
        return q_blocks, bufs, jnp.concatenate(locs, axis=0), jnp.concatenate(tids)

    diagonal = [(half, sides[half] + 1) for half in halves]
    straight, beside = [(half, sides[half]) for half in halves], [(half, 1) for half in halves]
    *outs, turn = attend(jnp.zeros((1,), jnp.int32), tiles, *operands(straight))
    *more, turn = attend(turn, tiles, *operands(diagonal + beside), shared=len(beside))
    sent = straight + diagonal + beside
    arrays = [swap(out, offset) for out, (_, offset) in zip(outs + more, sent)]
    columns = [head_of(half, offset) * WIDE for half, offset in sent]
    early = len(straight)
    result, _ = attend(
        turn, tiles, *operands([(half, 0) for half in halves]), [head_of(half, 0) * WIDE for half in halves],
        pieces=list(zip(arrays, columns))[:early],
    )
    return deliver(result, arrays[early:], columns[early:])


def solution(mesh):
    in_specs = (P(AXES, None), P(AXES, None), P(AXES, None), P(("kv", "pb"), None))
    sizes = tuple(mesh.shape[axis] for axis in AXES)
    return jax.shard_map(
        functools.partial(per_device, sizes),
        mesh=mesh, in_specs=in_specs, out_specs=P(AXES, None), check_vma=False,
    )
```
